32 devices in a mesh: cat: 16 (over z, y, core), tp: 2 (over x).
Axes of the slice: x: 2, y: 2, z: 4, core: 2. Of those that a mesh axis runs over, the one named last changes fastest.
Arguments:
- query_emb: bfloat16 [16384, 512], P('cat', 'tp'), may hold values from -100 to 100
- positive_emb: bfloat16 [16384, 512], P('cat', 'tp'), may hold values from -6 to 6
- item_hidden: bfloat16 [32768, 1024], P('cat', 'tp'), may hold values from -6 to 6
- item_weight: bfloat16 [1024, 512], P('tp'), may hold values from -0.1875 to 0.1875
- neg_blocks: int32 [64, 64], P('cat'), may hold values from 0 to 127, all different within a row
- block_home: int32 [128], replicated, may hold values from 0 to 127, each once
- sample_counts: int32 [32768], replicated, may hold values from 1 to 4096
Outputs:
- query_loss: float32 [16384], P('cat')
- query_grad: bfloat16 [16384, 512], P('cat', 'tp')
The draws below stay inside these ranges and needn't reach their ends.
Inputs may be any that keep to these rules, and one draw needn't show every extreme that they name: `neg_blocks`: each row names 64 different catalog blocks. `block_home`: each storage position once.
All inputs are finite; a program needn't handle non-finite values.
Results may differ from the reference program's by a relative error of at most 0.012.
Values may be sent and summed in bfloat16 or wider, within the bound.
A program may use at most 192 MiB of HBM per device.

```python
import math
import jax
import jax.numpy as jnp
from jax import lax

E = 512
HID = 1024
BLK = 256
NNEG = 64
QBLOCKS = 64
QUERIES = 16384
NB = 128
ITEMS = 32768


def draw_query_emb(key, part):
    key = jax.random.fold_in(key, 11)
    key_base, key_scale = jax.random.split(key, 2)
    base_vals = jnp.clip(jax.random.normal(key_base, (QUERIES, E), jnp.float32), -4.0, 4.0)
    row_scale = jnp.exp(jax.random.uniform(key_scale, (QUERIES, 1), jnp.float32, -0.7, 1.1))
    return jnp.clip(base_vals * row_scale, -100.0, 100.0).astype(jnp.bfloat16)


def with_ends(entries, own_key, smallest, largest):
    index_at = [jax.random.randint(jax.random.fold_in(own_key, axis), (), 0, length) for axis, length in enumerate(entries.shape)]
    main_axis = entries.shape.index(max(entries.shape))
    beside = index_at[:main_axis] + [(index_at[main_axis] + 1) % entries.shape[main_axis]] + index_at[main_axis + 1:]
    return entries.at[tuple(index_at)].set(smallest).at[tuple(beside)].set(largest)


def steps_of(own_key, dims, cuts, least, top_value):
    loudness = 1.0
    for axis_at, parts in cuts:
        heights = jax.random.uniform(jax.random.fold_in(jax.random.fold_in(own_key, 6), axis_at), (parts,), jnp.float32, least / len(cuts), top_value / len(cuts))
        loudness = loudness * jnp.repeat(jnp.exp(heights), dims[axis_at] // parts).reshape((-1,) + (1,) * (len(dims) - 1 - axis_at))
    return loudness


def distinct(own_key, rows, count, top, lift):
    ranking = jax.random.permutation(jax.random.fold_in(own_key, 1), count)
    boost = ranking
    for power in range(3):
        boost = boost * boost // count
    boost = boost * lift // count
    tickets = jax.random.randint(jax.random.fold_in(own_key, 2), (rows, count), 0, 4096) + boost
    sure = jax.random.permutation(jax.random.fold_in(own_key, 3), rows)[jnp.arange(count) % rows]
    tickets = jnp.where(jnp.arange(rows)[:, None] == sure[None, :], 1 << 14, tickets)
    priority = tickets * count + jnp.arange(count)
    return lax.top_k(priority.astype(jnp.int32), top)[1].astype(jnp.int32)


def bell_draw(key, dims, width, bound, cuts=(), dtype=jnp.bfloat16):
    level = steps_of(key, dims, cuts, -0.22, 0.18) if cuts else 1.0
    entries = jax.random.normal(key, dims, jnp.float32) * width * level
    return jnp.minimum(jnp.maximum(entries, -bound), bound).astype(dtype)


def setup_inputs(seed: int = 0) -> dict:
    splits = jax.random.split(jax.random.key(seed), 8)
    return {
        "query_emb": draw_query_emb(jax.random.fold_in(splits[7], 71), 0),
        "positive_emb": bell_draw(splits[1], (QUERIES, E), 1.0, 6.0, ((0, 16), (1, 2))),
        "item_hidden": bell_draw(splits[2], (ITEMS, HID), 1.0, 6.0, ((0, 16), (1, 2))),
        "item_weight": bell_draw(splits[3], (HID, E), HID ** -0.5, 0.1875, ((0, 2),)),
        "neg_blocks": distinct(splits[4], QBLOCKS, NB, NNEG, 8192),
        "block_home": jax.random.permutation(splits[5], NB).astype(jnp.int32),
        "sample_counts": with_ends(jax.random.randint(splits[6], (ITEMS,), 1, 4097), jax.random.fold_in(splits[6], 1), 1, 4096).astype(jnp.int32),
    }


def reference(query_emb, positive_emb, item_hidden, item_weight, neg_blocks, block_home, sample_counts):
    score_scale = 2.0 / math.sqrt(E)
    item_vec = jnp.dot(item_hidden, item_weight, preferred_element_type=jnp.float32).astype(jnp.bfloat16)
    log_q = jnp.log(sample_counts.astype(jnp.float32))
    vec_blocks = item_vec.reshape(NB, BLK, E)
    logq_blocks = log_q.reshape(NB, BLK)
    home_ids = block_home[neg_blocks].astype(jnp.int32)
    query_blocks = query_emb.reshape(QBLOCKS, BLK, E)
    positive_blocks = positive_emb.reshape(QBLOCKS, BLK, E)

    def one_block(inputs):
        query_block, positive_block, block_ids = inputs
        picked = vec_blocks[block_ids].reshape(NNEG * BLK, E)
        picked_q = logq_blocks[block_ids].reshape(NNEG * BLK)
        scores = score_scale * jnp.dot(query_block, picked.T, preferred_element_type=jnp.float32) - picked_q[None, :]
        pos_score = score_scale * lax.optimization_barrier(jnp.sum(query_block.astype(jnp.float32) * positive_block.astype(jnp.float32), axis=1))
        run_max = jnp.maximum(lax.optimization_barrier(jnp.max(scores, axis=1)), pos_score)
        run_sum = lax.optimization_barrier(jnp.sum(jnp.exp(scores - run_max[:, None]), axis=1)) + jnp.exp(pos_score - run_max)
        log_total = run_max + jnp.log(run_sum)
        weights = jnp.exp(scores - log_total[:, None]).astype(jnp.bfloat16)
        weighted = jnp.dot(weights, picked, preferred_element_type=jnp.float32)
        pos_weight = jnp.exp(pos_score - log_total)
        query_grad = score_scale * (weighted + (pos_weight - 1.0)[:, None] * positive_block.astype(jnp.float32))
        return (log_total - pos_score, query_grad.astype(jnp.bfloat16))
    query_loss, query_grad = lax.map(one_block, (query_blocks, positive_blocks, home_ids))
    return (query_loss.reshape(QUERIES), query_grad.reshape(QUERIES, E))
```

```python
import functools
import math

import jax
import jax.numpy as jnp
from jax import lax
from jax.experimental import pallas as pl
from jax.experimental.pallas import tpu as pltpu
from jax.sharding import PartitionSpec as P

BLK = 256
LANES = 128
CHUNKS = 2
NEG = -1e30
LOG2E = math.log2(math.e)
LN2 = math.log(2.0)


def lookup(index, values):
    result = values[0]
    for place, value in enumerate(values[1:], 1):
        result = jnp.where(index == place, value, result)
    return result


def nearest(count):
    return [sorted(range(count), key=lambda other: abs(other - at)) for at in range(count)]


def kernel(
    sizes, scale,
    q_ref, pos_ref, h_ref, w_ref, bias_ref, loss_ref, grad_ref,
    table, hbuf, wbuf, qbuf, qfull, run_max, run_sum, acc, osend, orecv, stats,
    local_sem, w_send, w_recv, q_send, q_recv, h_send, h_recv,
    t_send, t_recv, o_send, o_recv, s_send, s_recv,
):
    tp, rows_a, rows_b = sizes
    me_t = lax.axis_index("tp")
    me_c = lax.axis_index("cat")
    core = me_c % 2
    at_b = (me_c // 2) % rows_b
    at_a = me_c // (2 * rows_b)
    queries, width = q_ref.shape
    feats = table.shape[2]
    chunk_rows = table.shape[1]
    own_blocks, _, _ = h_ref.shape
    sub_rows = BLK // tp
    groups = queries // BLK
    part_blocks = own_blocks // CHUNKS

    def cat_of(a, b, k):
        return (a * rows_b + b) * 2 + k

    ways = [
        (at_a > 0, cat_of(at_a - 1, at_b, core)),
        (at_a < rows_a - 1, cat_of(at_a + 1, at_b, core)),
        (at_b > 0, cat_of(at_a, at_b - 1, core)),
        (at_b < rows_b - 1, cat_of(at_a, at_b + 1, core)),
        (at_a >= 0, cat_of(at_a, at_b, 1 - core)),
    ]
    peers = [lax.rem(me_t + d, tp) for d in range(1, tp)]

    barrier = pltpu.get_barrier_semaphore()
    total = jnp.int32(tp - 1)
    for peer in peers:
        pl.semaphore_signal(barrier, inc=1, device_id={"tp": peer}, device_id_type=pl.DeviceIdType.MESH)
    for there, target in ways:
        @pl.when(there)
        def _():
            pl.semaphore_signal(barrier, inc=1, device_id={"cat": target}, device_id_type=pl.DeviceIdType.MESH)
        total = total + there.astype(jnp.int32)
    pl.semaphore_wait(barrier, total)

    def across(src, dst, send, recv, peer):
        return pltpu.make_async_remote_copy(
            src_ref=src, dst_ref=dst, send_sem=send, recv_sem=recv,
            device_id={"tp": peer}, device_id_type=pl.DeviceIdType.MESH,
        )

    def w_copy(slot, d, peer):
        return across(w_ref, wbuf.at[slot], w_send.at[d], w_recv.at[slot], peer)

    def q_copy(slot, d, peer):
        return across(q_ref, qbuf.at[slot], q_send.at[d], q_recv.at[slot], peer)

    def h_part(part, owner):
        return h_ref.at[
            pl.ds(part * part_blocks, part_blocks),
            pl.ds(pl.multiple_of(owner * sub_rows, sub_rows), sub_rows),
        ]

    def h_copy(slot, d, part, peer):
        return across(h_part(part, peer), hbuf.at[slot, part], h_send.at[d, part], h_recv.at[slot, part], peer)

    for d, peer in enumerate(peers):
        w_copy(me_t, d, peer).start()
    for part in range(CHUNKS):
        for d, peer in enumerate(peers):
            h_copy(me_t, d, part, peer).start()
    for d, peer in enumerate(peers):
        q_copy(me_t, d, peer).start()
    own = [
        pltpu.make_async_copy(w_ref, wbuf.at[me_t], local_sem.at[0]),
        pltpu.make_async_copy(q_ref, qbuf.at[me_t], local_sem.at[1]),
    ] + [
        pltpu.make_async_copy(h_part(part, me_t), hbuf.at[me_t, part], local_sem.at[2 + part])
        for part in range(CHUNKS)
    ]
    for copy in own:
        copy.start()

    run_max[...] = jnp.full_like(run_max, NEG)
    run_sum[...] = jnp.zeros_like(run_sum)
    acc[...] = jnp.zeros_like(acc)
    diag = lax.broadcasted_iota(jnp.int32, (LANES, LANES), 0) == lax.broadcasted_iota(
        jnp.int32, (LANES, LANES), 1
    )
    stat_rows = queries // LANES

    def as_row(column):
        return jnp.sum(jnp.where(diag, column, 0.0), axis=0, keepdims=True)

    def as_column(row):
        return jnp.sum(jnp.where(diag, row, 0.0), axis=1, keepdims=True)

    def table_copy(slot, way):
        return pltpu.make_async_remote_copy(
            src_ref=table.at[slot], dst_ref=table.at[slot],
            send_sem=t_send.at[slot, way], recv_sem=t_recv.at[slot],
            device_id={"cat": ways[way][1]}, device_id_type=pl.DeviceIdType.MESH,
        )

    def sends(a, b):
        return [
            ways[0][0] & (b == at_b) & (a >= at_a),
            ways[1][0] & (b == at_b) & (a <= at_a),
            ways[2][0] & (b >= at_b),
            ways[3][0] & (b <= at_b),
            ways[4][0],
        ]

    def hand_on(a, b, part, act):
        slot = cat_of(a, b, core) * CHUNKS + part
        for way, wanted in enumerate(sends(a, b)):
            @pl.when(wanted)
            def _():
                act(table_copy(slot, way))

    own[0].wait()
    for d, peer in enumerate(peers):
        w_copy(peer, d, peer).wait_recv()
    for part in range(CHUNKS):
        own[2 + part].wait()
        for d, peer in enumerate(peers):
            h_copy(peer, d, part, peer).wait_recv()
        vec = jnp.zeros((chunk_rows, feats), jnp.float32)
        for t in range(tp):
            vec = vec + jnp.dot(
                hbuf[t, part].reshape(chunk_rows, hbuf.shape[-1]), wbuf[t],
                preferred_element_type=jnp.float32,
            )
        table[me_c * CHUNKS + part] = vec.astype(jnp.bfloat16)
        hand_on(at_a, at_b, part, lambda copy: copy.start())

    own[1].wait()
    for d, peer in enumerate(peers):
        q_copy(peer, d, peer).wait_recv()
    for t in range(tp):
        qfull[:, t * width:(t + 1) * width] = qbuf[t]
    for row in range(stat_rows):
        rows = slice(row * LANES, (row + 1) * LANES)
        product = qbuf[me_t, rows, :].astype(jnp.float32) * pos_ref[rows, :].astype(jnp.float32)
        stats[me_t, stat_rows + row:stat_rows + row + 1, :] = as_row(
            jnp.sum(product, axis=1, keepdims=True)
        )

    def attend(slot):
        items = table[slot]
        for g in range(groups):
            rows = slice(g * BLK, (g + 1) * BLK)
            raw = lax.dot_general(
                qfull[rows, :], items, (((1,), (1,)), ((), ())), preferred_element_type=jnp.float32
            )
            tiles = [
                raw[:, i * LANES:(i + 1) * LANES] * (scale * LOG2E) + bias_ref[g, slot, i:i + 1, :]
                for i in range(chunk_rows // LANES)
            ]
            top = functools.reduce(jnp.maximum, tiles)
            old_max = run_max[rows, :]
            new_max = jnp.maximum(old_max, jnp.max(top, axis=1, keepdims=True))
            fade = jnp.exp2(old_max - new_max)
            tiles = [jnp.exp2(tile - new_max) for tile in tiles]
            run_max[rows, :] = new_max
            run_sum[rows, :] = run_sum[rows, :] * fade + functools.reduce(jnp.add, tiles)
            weights = jnp.concatenate([tile.astype(jnp.bfloat16) for tile in tiles], axis=1)
            part = jnp.dot(weights, items, preferred_element_type=jnp.float32)
            for i in range(feats // LANES):
                cols = slice(i * LANES, (i + 1) * LANES)
                acc[rows, cols] = acc[rows, cols] * fade + part[:, cols]

    ranks = sorted(
        [(i, j) for i in range(rows_a) for j in range(rows_b)], key=lambda r: (r[0] + r[1], r[1])
    )
    near_a, near_b = nearest(rows_a), nearest(rows_b)

    def source(index):
        rank_a = lookup(index, [r[0] for r in ranks])
        rank_b = lookup(index, [r[1] for r in ranks])
        a = lookup(rank_a * rows_a + at_a, [near_a[p][r] for r in range(rows_a) for p in range(rows_a)])
        b = lookup(rank_b * rows_b + at_b, [near_b[p][r] for r in range(rows_b) for p in range(rows_b)])
        return a, b

    @pl.loop(0, len(ranks) * CHUNKS)
    def _(step):
        index, part = step // CHUNKS, step % CHUNKS
        a, b = source(index)

        @pl.when(index > 0)
        def _():
            table_copy(cat_of(a, b, core) * CHUNKS + part, 4).wait_recv()
            hand_on(a, b, part, lambda copy: copy.start())

        @pl.loop(0, 2)
        def _(other):
            slot = cat_of(a, b, (core + other) % 2) * CHUNKS + part

            @pl.when(other > 0)
            def _():
                table_copy(slot, 4).wait_recv()

            attend(slot)

    def o_copy(slot, d, g, peer):
        rows = pl.ds(g * BLK, BLK)
        return across(osend.at[d, rows], orecv.at[slot, rows], o_send.at[d, g], o_recv.at[slot, g], peer)

    def s_copy(slot, d, peer):
        return across(stats.at[slot], stats.at[slot], s_send.at[d], s_recv.at[slot], peer)

    for g in range(groups):
        rows = slice(g * BLK, (g + 1) * BLK)
        norm = jnp.sum(run_sum[rows, :], axis=1, keepdims=True)
        lse = run_max[rows, 0:1] + jnp.log2(norm)
        inverse = 1.0 / norm
        for i in range(BLK // LANES):
            row = g * (BLK // LANES) + i
            stats[me_t, row:row + 1, :] = as_row(lse[i * LANES:(i + 1) * LANES, :])
        for d, peer in enumerate(peers):
            cols = pl.ds(pl.multiple_of(peer * width, LANES), width)
            osend[d, rows, :] = (acc[rows, cols] * inverse).astype(jnp.bfloat16)
            o_copy(me_t, d, g, peer).start()
        cols = pl.ds(pl.multiple_of(me_t * width, LANES), width)
        acc[rows, cols] = acc[rows, cols] * inverse
    for d, peer in enumerate(peers):
        s_copy(me_t, d, peer).start()
    for d, peer in enumerate(peers):
        s_copy(peer, d, peer).wait_recv()
    for g in range(groups):
        for d, peer in enumerate(peers):
            o_copy(peer, d, g, peer).wait_recv()
        for i in range(BLK // LANES):
            row = g * (BLK // LANES) + i
            rows = slice(row * LANES, (row + 1) * LANES)
            pos = sum(stats[t, stat_rows + row:stat_rows + row + 1, :] for t in range(tp)) * (scale * LOG2E)
            lses = [stats[t, row:row + 1, :] for t in range(tp)]
            top = functools.reduce(jnp.maximum, lses + [pos])
            log_total = top + jnp.log2(sum(jnp.exp2(v - top) for v in lses + [pos]))
            loss_ref[row:row + 1, :] = (log_total - pos) * LN2
            shift = as_column(log_total)
            cols = pl.ds(pl.multiple_of(me_t * width, LANES), width)
            grad = acc[rows, cols] * jnp.exp2(as_column(stats[me_t, row:row + 1, :]) - shift)
            for peer in peers:
                share = jnp.exp2(as_column(stats[peer, row:row + 1, :]) - shift)
                grad = grad + orecv[peer, rows, :].astype(jnp.float32) * share
            pos_weight = jnp.exp2(as_column(pos - log_total)) - 1.0
            grad = grad + pos_weight * pos_ref[rows, :].astype(jnp.float32)
            grad_ref[rows, :] = (scale * grad).astype(jnp.bfloat16)

    for d, peer in enumerate(peers):
        w_copy(me_t, d, peer).wait_send()
        q_copy(me_t, d, peer).wait_send()
        for part in range(CHUNKS):
            h_copy(me_t, d, part, peer).wait_send()
        for g in range(groups):
            o_copy(me_t, d, g, peer).wait_send()
        s_copy(me_t, d, peer).wait_send()

    @pl.loop(0, len(ranks) * CHUNKS)
    def _(step):
        index, part = step // CHUNKS, step % CHUNKS
        a, b = source(index)
        hand_on(a, b, part, lambda copy: copy.wait_send())


def local(query_emb, positive_emb, item_hidden, item_weight, neg_blocks, block_home, sample_counts):
    tp = lax.axis_size("tp")
    cats = lax.axis_size("cat")
    rows_a = 4
    rows_b = cats // 2 // rows_a
    me_t = lax.axis_index("tp")
    queries, width = query_emb.shape
    hid, feats = item_weight.shape
    own_blocks = item_hidden.shape[0] // BLK
    sub_rows = BLK // tp
    total_blocks = block_home.shape[0]
    groups = neg_blocks.shape[0]
    chunk_rows = own_blocks * sub_rows // CHUNKS
    slots = cats * CHUNKS
    scale = 2.0 / math.sqrt(feats)

    ids = jnp.arange(total_blocks, dtype=jnp.int32)
    chosen = jnp.any(neg_blocks[:, :, None] == ids, axis=1)
    stored = jnp.any(chosen[:, :, None] & (block_home[:, None] == ids), axis=1)
    log_q = jnp.log(sample_counts.astype(jnp.float32)).reshape(total_blocks, tp, sub_rows)
    log_q = lax.dynamic_index_in_dim(log_q, me_t, 1, keepdims=False)
    bias = jnp.where(stored[:, :, None], log_q * -LOG2E, NEG).reshape(
        groups, slots, chunk_rows // LANES, LANES
    )
    vmem = pl.BlockSpec(memory_space=pltpu.VMEM)
    hbm = pl.BlockSpec(memory_space=pl.ANY)
    dma = pltpu.SemaphoreType.DMA
    others = max(tp - 1, 1)
    flops = 4 * queries * slots * chunk_rows * feats
    loss, grad = pl.pallas_call(
        functools.partial(kernel, (tp, rows_a, rows_b), scale),
        out_shape=(
            jax.ShapeDtypeStruct((queries // LANES, LANES), jnp.float32),
            jax.ShapeDtypeStruct((queries, width), jnp.bfloat16),
        ),
        in_specs=[hbm, vmem, hbm, hbm, vmem],
        out_specs=(vmem, vmem),
        scratch_shapes=[
            pltpu.VMEM((slots, chunk_rows, feats), jnp.bfloat16),
            pltpu.VMEM((tp, CHUNKS, own_blocks // CHUNKS, sub_rows, hid), jnp.bfloat16),
            pltpu.VMEM((tp, hid, feats), jnp.bfloat16),
            pltpu.VMEM((tp, queries, width), jnp.bfloat16),
            pltpu.VMEM((queries, feats), jnp.bfloat16),
            pltpu.VMEM((queries, LANES), jnp.float32),
            pltpu.VMEM((queries, LANES), jnp.float32),
            pltpu.VMEM((queries, feats), jnp.float32),
            pltpu.VMEM((others, queries, width), jnp.bfloat16),
            pltpu.VMEM((tp, queries, width), jnp.bfloat16),
            pltpu.VMEM((tp, 2 * queries // LANES, LANES), jnp.float32),
            dma((2 + CHUNKS,)),
            dma((others,)), dma((tp,)),
            dma((others,)), dma((tp,)),
            dma((others, CHUNKS)), dma((tp, CHUNKS)),
            dma((slots, 5)), dma((slots,)),
            dma((others, groups)), dma((tp, groups)),
            dma((others,)), dma((tp,)),
        ],
        compiler_params=pltpu.CompilerParams(
            collective_id=0, has_side_effects=True, vmem_limit_bytes=48 * 1024 * 1024
        ),
        cost_estimate=pl.CostEstimate(
            flops=flops, bytes_accessed=8 * 1024 * 1024, transcendentals=queries * slots * chunk_rows
        ),
    )(
        query_emb, positive_emb, item_hidden.reshape(own_blocks, BLK, hid), item_weight, bias,
    )
    return loss.reshape(-1), grad


def solution(mesh):
    placed = (
        P("cat", "tp"),
        P("cat", "tp"),
        P("cat", "tp"),
        P("tp", None),
        P("cat", None),
        P(),
        P(),
    )
    return jax.shard_map(
        local, mesh=mesh, in_specs=placed, out_specs=(P("cat"), P("cat", "tp")), check_vma=False
    )
```

```python
import functools
import math

import jax
import jax.numpy as jnp
from jax import lax
from jax.experimental import pallas as pl
from jax.experimental.pallas import tpu as pltpu
from jax.sharding import PartitionSpec as P

BLK = 256
LANES = 128
CHUNKS = 4
AHEAD = 3
NEG = -1e30
LOG2E = math.log2(math.e)
LN2 = math.log(2.0)


def lookup(index, values):
    result = values[0]
    for place, value in enumerate(values[1:], 1):
        result = jnp.where(index == place, value, result)
    return result


def nearest(count):
    return [sorted(range(count), key=lambda other: abs(other - at)) for at in range(count)]


def kernel(
    sizes, scale,
    q_ref, pos_in, h_ref, w_ref, bias_ref, loss_ref, grad_ref,
    table, hbuf, wbuf, qbuf, pos_ref, qfull, run_max, run_sum, acc, osend, orecv, stats,
    local_sem, w_send, w_recv, w_pass, q_send, q_recv, h_send, h_recv,
    t_send, t_recv, o_send, o_recv, s_send, s_recv,
):
    tp, rows_a, rows_b = sizes
    me_t = lax.axis_index("tp")
    me_c = lax.axis_index("cat")
    core = me_c % 2
    at_b = (me_c // 2) % rows_b
    at_a = me_c // (2 * rows_b)
    queries, width = q_ref.shape
    feats = table.shape[3]
    chunk_rows = table.shape[2]
    own_blocks, _, _ = h_ref.shape
    sub_rows = BLK // tp
    groups = queries // BLK
    part_blocks = own_blocks // CHUNKS
    half = wbuf.shape[2]

    def cat_of(a, b, k):
        return (a * rows_b + b) * 2 + k

    ways = [
        (at_a > 0, cat_of(at_a - 1, at_b, core)),
        (at_a < rows_a - 1, cat_of(at_a + 1, at_b, core)),
        (at_b > 0, cat_of(at_a, at_b - 1, core)),
        (at_b < rows_b - 1, cat_of(at_a, at_b + 1, core)),
        (at_a >= 0, cat_of(at_a, at_b, 1 - core)),
    ]
    peers = [lax.rem(me_t + d, tp) for d in range(1, tp)]

    barrier = pltpu.get_barrier_semaphore()
    total = jnp.int32(tp - 1)
    for peer in peers:
        pl.semaphore_signal(barrier, inc=1, device_id={"tp": peer}, device_id_type=pl.DeviceIdType.MESH)
    for there, target in ways:
        @pl.when(there)
        def _():
            pl.semaphore_signal(barrier, inc=1, device_id={"cat": target}, device_id_type=pl.DeviceIdType.MESH)
        total = total + there.astype(jnp.int32)
    pl.semaphore_wait(barrier, total)

    def across(src, dst, send, recv, peer):
        return pltpu.make_async_remote_copy(
            src_ref=src, dst_ref=dst, send_sem=send, recv_sem=recv,
            device_id={"tp": peer}, device_id_type=pl.DeviceIdType.MESH,
        )

    def w_half(k):
        return w_ref.at[pl.ds(pl.multiple_of(k * half, half), half)]

    def w_copy(slot, d, peer):
        return across(w_half(core), wbuf.at[slot, core], w_send.at[d], w_recv.at[slot, core], peer)

    def w_hand(slot, k, d):
        return pltpu.make_async_remote_copy(
            src_ref=wbuf.at[slot, k], dst_ref=wbuf.at[slot, k],
            send_sem=w_pass.at[d], recv_sem=w_recv.at[slot, k],
            device_id={"cat": ways[4][1]}, device_id_type=pl.DeviceIdType.MESH,
        )

    def q_copy(slot, d, peer):
        return across(q_ref, qbuf.at[slot], q_send.at[d], q_recv.at[slot], peer)

    def h_part(part, owner):
        return h_ref.at[
            pl.ds(part * part_blocks, part_blocks),
            pl.ds(pl.multiple_of(owner * sub_rows, sub_rows), sub_rows),
        ]

    def h_copy(slot, d, part, peer):
        return across(h_part(part, peer), hbuf.at[slot, part], h_send.at[d, part], h_recv.at[slot, part], peer)

    for d, peer in enumerate(peers):
        w_copy(me_t, d, peer).start()
        h_copy(me_t, d, 0, peer).start()
    own = [
        pltpu.make_async_copy(w_half(0), wbuf.at[me_t, 0], local_sem.at[0]),
        pltpu.make_async_copy(w_half(1), wbuf.at[me_t, 1], local_sem.at[1]),
        pltpu.make_async_copy(q_ref, qbuf.at[me_t], local_sem.at[2]),
        pltpu.make_async_copy(pos_in, pos_ref, local_sem.at[3]),
    ]

    def own_part(part):
        return pltpu.make_async_copy(h_part(part, me_t), hbuf.at[me_t, part], local_sem.at[4 + part])

    for copy in own + [own_part(part) for part in range(CHUNKS)]:
        copy.start()

    run_max[...] = jnp.full_like(run_max, NEG)
    run_sum[...] = jnp.zeros_like(run_sum)
    acc[...] = jnp.zeros_like(acc)
    diag = lax.broadcasted_iota(jnp.int32, (LANES, LANES), 0) == lax.broadcasted_iota(
        jnp.int32, (LANES, LANES), 1
    )
    stat_rows = queries // LANES

    def as_row(column):
        return jnp.sum(jnp.where(diag, column, 0.0), axis=0, keepdims=True)

    def as_column(row):
        return jnp.sum(jnp.where(diag, row, 0.0), axis=1, keepdims=True)

    def pair_of(a, b, part):
        return (a * rows_b + b) * CHUNKS + part

    def table_copy(pair, k, way):
        return pltpu.make_async_remote_copy(
            src_ref=table.at[pair, k], dst_ref=table.at[pair, k],
            send_sem=t_send.at[pair, way], recv_sem=t_recv.at[pair, k],
            device_id={"cat": ways[way][1]}, device_id_type=pl.DeviceIdType.MESH,
        )

    def sends(a, b, part):
        b_first = (part == 2) & (a != rows_a // 2)
        along_a = b_first | (b == at_b)
        along_b = jnp.logical_not(b_first) | (a == at_a)
        return [
            ways[0][0] & along_a & (a >= at_a),
            ways[1][0] & along_a & (a <= at_a),
            ways[2][0] & along_b & (b >= at_b),
            ways[3][0] & along_b & (b <= at_b),
            ways[4][0],
        ]

    def hand_on(a, b, part, act):
        pair = pair_of(a, b, part)
        for way, wanted in enumerate(sends(a, b, part)):
            @pl.when(wanted)
            def _():
                act(table_copy(pair, core, way))

    order = sorted(
        [(i, j, p) for p in range(CHUNKS) for i in range(rows_a) for j in range(rows_b)],
        key=lambda r: (r[0] + r[1] + (rows_a - 0.5) * r[2], r[1]),
    )
    near_a, near_b = nearest(rows_a), nearest(rows_b)

    def source(step):
        rank_a, rank_b, part = (lookup(step, [r[i] for r in order]) for i in range(3))
        a = lookup(rank_a * rows_a + at_a, [near_a[p][r] for r in range(rows_a) for p in range(rows_a)])
        b = lookup(rank_b * rows_b + at_b, [near_b[p][r] for r in range(rows_b) for p in range(rows_b)])
        return a, b, part

    def advance(step):
        a, b, part = source(step)
        mine = (a == at_a) & (b == at_b)

        @pl.when(mine)
        def _():
            own_part(part).wait()
            for d, peer in enumerate(peers):
                h_copy(peer, d, part, peer).wait_recv()
            vec = jnp.zeros((chunk_rows, feats), jnp.float32)
            for t in range(tp):
                for k in range(2):
                    hidden = hbuf[t, part, :, :, k * half:(k + 1) * half]
                    vec = vec + jnp.dot(
                        hidden.reshape(chunk_rows, half), wbuf[t, k], preferred_element_type=jnp.float32
                    )
            table[pair_of(a, b, part), core] = vec.astype(jnp.bfloat16)

        @pl.when(jnp.logical_not(mine))
        def _():
            table_copy(pair_of(a, b, part), core, 4).wait_recv()

        hand_on(a, b, part, lambda copy: copy.start())

    def partner(step):
        pair = pair_of(*source(step))
        table_copy(pair, 1 - core, 4).wait_recv()
        return pair

    own[0].wait()
    own[1].wait()
    for d, peer in enumerate(peers):
        w_copy(peer, d, peer).wait_recv()
        w_hand(peer, core, d).start()
    for d, peer in enumerate(peers):
        w_hand(peer, 1 - core, d).wait_recv()
    advance(jnp.int32(0))
    for d, peer in enumerate(peers):
        q_copy(me_t, d, peer).start()
    for d, peer in enumerate(peers):
        h_copy(me_t, d, 1, peer).start()

    @pl.loop(1, AHEAD)
    def _(step):
        advance(step)

    own[2].wait()
    own[3].wait()
    for d, peer in enumerate(peers):
        q_copy(peer, d, peer).wait_recv()
    for part in range(2, CHUNKS):
        for d, peer in enumerate(peers):
            h_copy(me_t, d, part, peer).start()
    for t in range(tp):
        qfull[:, t * width:(t + 1) * width] = qbuf[t]

    def attend(pair, wanted):
        items = table[pair].reshape(2 * chunk_rows, feats)
        for g in wanted:
            rows = slice(g * BLK, (g + 1) * BLK)
            raw = lax.dot_general(
                qfull[rows, :], items, (((1,), (1,)), ((), ())), preferred_element_type=jnp.float32
            )
            tiles = [
                raw[:, i * LANES:(i + 1) * LANES] * (scale * LOG2E) + bias_ref[g, pair, i:i + 1, :]
                for i in range(2 * chunk_rows // LANES)
            ]
            top = functools.reduce(jnp.maximum, tiles)
            old_max = run_max[rows, :]
            new_max = jnp.maximum(old_max, jnp.max(top, axis=1, keepdims=True))
            fade = jnp.exp2(old_max - new_max)
            tiles = [jnp.exp2(tile - new_max) for tile in tiles]
            run_max[rows, :] = new_max
            run_sum[rows, :] = run_sum[rows, :] * fade + functools.reduce(jnp.add, tiles)
            weights = jnp.concatenate([tile.astype(jnp.bfloat16) for tile in tiles], axis=1)
            part = jnp.dot(weights, items, preferred_element_type=jnp.float32)
            for i in range(feats // LANES):
                cols = slice(i * LANES, (i + 1) * LANES)
                acc[rows, cols] = acc[rows, cols] * fade + part[:, cols]

    steps = len(order)

    @pl.loop(0, steps - 1)
    def _(step):
        @pl.when(step + AHEAD < steps)
        def _():
            advance(step + AHEAD)

        attend(partner(step), range(groups))

    for row in range(stat_rows):
        rows = slice(row * LANES, (row + 1) * LANES)
        product = qbuf[me_t, rows, :].astype(jnp.float32) * pos_ref[rows, :].astype(jnp.float32)
        stats[me_t, stat_rows + row:stat_rows + row + 1, :] = as_row(
            jnp.sum(product, axis=1, keepdims=True)
        )
    last = partner(jnp.int32(steps - 1))

    def o_copy(slot, d, g, peer):
        rows = pl.ds(g * BLK, BLK)
        return across(osend.at[d, rows], orecv.at[slot, rows], o_send.at[d, g], o_recv.at[slot, g], peer)

    def s_copy(slot, d, peer):
        return across(stats.at[slot], stats.at[slot], s_send.at[d], s_recv.at[slot], peer)

    for g in range(groups):
        attend(last, [g])
        rows = slice(g * BLK, (g + 1) * BLK)
        norm = jnp.sum(run_sum[rows, :], axis=1, keepdims=True)
        lse = run_max[rows, 0:1] + jnp.log2(norm)
        inverse = 1.0 / norm
        for i in range(BLK // LANES):
            row = g * (BLK // LANES) + i
            stats[me_t, row:row + 1, :] = as_row(lse[i * LANES:(i + 1) * LANES, :])
        for d, peer in enumerate(peers):
            cols = pl.ds(pl.multiple_of(peer * width, LANES), width)
            osend[d, rows, :] = (acc[rows, cols] * inverse).astype(jnp.bfloat16)
            o_copy(me_t, d, g, peer).start()
        cols = pl.ds(pl.multiple_of(me_t * width, LANES), width)
        acc[rows, cols] = acc[rows, cols] * inverse
    for d, peer in enumerate(peers):
        s_copy(me_t, d, peer).start()
    for d, peer in enumerate(peers):
        s_copy(peer, d, peer).wait_recv()
    for g in range(groups):
        for d, peer in enumerate(peers):
            o_copy(peer, d, g, peer).wait_recv()
        for i in range(BLK // LANES):
            row = g * (BLK // LANES) + i
            rows = slice(row * LANES, (row + 1) * LANES)
            pos = sum(stats[t, stat_rows + row:stat_rows + row + 1, :] for t in range(tp)) * (scale * LOG2E)
            lses = [stats[t, row:row + 1, :] for t in range(tp)]
            top = functools.reduce(jnp.maximum, lses + [pos])
            log_total = top + jnp.log2(sum(jnp.exp2(v - top) for v in lses + [pos]))
            loss_ref[row:row + 1, :] = (log_total - pos) * LN2
            shift = as_column(log_total)
            cols = pl.ds(pl.multiple_of(me_t * width, LANES), width)
            grad = acc[rows, cols] * jnp.exp2(as_column(stats[me_t, row:row + 1, :]) - shift)
            for peer in peers:
                share = jnp.exp2(as_column(stats[peer, row:row + 1, :]) - shift)
                grad = grad + orecv[peer, rows, :].astype(jnp.float32) * share
            pos_weight = jnp.exp2(as_column(pos - log_total)) - 1.0
            grad = grad + pos_weight * pos_ref[rows, :].astype(jnp.float32)
            grad_ref[rows, :] = (scale * grad).astype(jnp.bfloat16)

    for d, peer in enumerate(peers):
        w_copy(me_t, d, peer).wait_send()
        w_hand(peer, core, d).wait_send()
        q_copy(me_t, d, peer).wait_send()
        for part in range(CHUNKS):
            h_copy(me_t, d, part, peer).wait_send()
        for g in range(groups):
            o_copy(me_t, d, g, peer).wait_send()
        s_copy(me_t, d, peer).wait_send()

    @pl.loop(0, steps)
    def _(step):
        hand_on(*source(step), lambda copy: copy.wait_send())


def local(query_emb, positive_emb, item_hidden, item_weight, neg_blocks, block_home, sample_counts):
    tp = lax.axis_size("tp")
    cats = lax.axis_size("cat")
    rows_a = 4
    rows_b = cats // 2 // rows_a
    me_t = lax.axis_index("tp")
    queries, width = query_emb.shape
    hid, feats = item_weight.shape
    own_blocks = item_hidden.shape[0] // BLK
    sub_rows = BLK // tp
    total_blocks = block_home.shape[0]
    groups = neg_blocks.shape[0]
    chunk_rows = own_blocks * sub_rows // CHUNKS
    pairs = cats // 2 * CHUNKS
    scale = 2.0 / math.sqrt(feats)

    ids = jnp.arange(total_blocks, dtype=jnp.int32)
    chosen = jnp.any(neg_blocks[:, :, None] == ids, axis=1)
    stored = jnp.any(chosen[:, :, None] & (block_home[:, None] == ids), axis=1)
    log_q = jnp.log(sample_counts.astype(jnp.float32)).reshape(total_blocks, tp, sub_rows)
    log_q = lax.dynamic_index_in_dim(log_q, me_t, 1, keepdims=False)
    bias = jnp.where(stored[:, :, None], log_q * -LOG2E, NEG)
    bias = (
        bias.reshape(groups, cats // 2, 2, CHUNKS, chunk_rows)
        .transpose(0, 1, 3, 2, 4)
        .reshape(groups, pairs, 2 * chunk_rows // LANES, LANES)
    )
    vmem = pl.BlockSpec(memory_space=pltpu.VMEM)
    hbm = pl.BlockSpec(memory_space=pl.ANY)
    dma = pltpu.SemaphoreType.DMA
    others = max(tp - 1, 1)
    pairwise = queries * pairs * 2 * chunk_rows
    loss, grad = pl.pallas_call(
        functools.partial(kernel, (tp, rows_a, rows_b), scale),
        out_shape=(
            jax.ShapeDtypeStruct((queries // LANES, LANES), jnp.float32),
            jax.ShapeDtypeStruct((queries, width), jnp.bfloat16),
        ),
        in_specs=[hbm, hbm, hbm, hbm, vmem],
        out_specs=(vmem, vmem),
        scratch_shapes=[
            pltpu.VMEM((pairs, 2, chunk_rows, feats), jnp.bfloat16),
            pltpu.VMEM((tp, CHUNKS, own_blocks // CHUNKS, sub_rows, hid), jnp.bfloat16),
            pltpu.VMEM((tp, 2, hid // 2, feats), jnp.bfloat16),
            pltpu.VMEM((tp, queries, width), jnp.bfloat16),
            pltpu.VMEM((queries, width), jnp.bfloat16),
            pltpu.VMEM((queries, feats), jnp.bfloat16),
            pltpu.VMEM((queries, LANES), jnp.float32),
            pltpu.VMEM((queries, LANES), jnp.float32),
            pltpu.VMEM((queries, feats), jnp.float32),
            pltpu.VMEM((others, queries, width), jnp.bfloat16),
            pltpu.VMEM((tp, queries, width), jnp.bfloat16),
            pltpu.VMEM((tp, 2 * queries // LANES, LANES), jnp.float32),
            dma((4 + CHUNKS,)),
            dma((others,)), dma((tp, 2)), dma((others,)),
            dma((others,)), dma((tp,)),
            dma((others, CHUNKS)), dma((tp, CHUNKS)),
            dma((pairs, 5)), dma((pairs, 2)),
            dma((others, groups)), dma((tp, groups)),
            dma((others,)), dma((tp,)),
        ],
        compiler_params=pltpu.CompilerParams(
            collective_id=0, has_side_effects=True, vmem_limit_bytes=60 * 1024 * 1024
        ),
        cost_estimate=pl.CostEstimate(
            flops=4 * pairwise * feats, bytes_accessed=8 * 1024 * 1024, transcendentals=pairwise
        ),
    )(
        query_emb, positive_emb, item_hidden.reshape(own_blocks, BLK, hid), item_weight, bias,
    )
    return loss.reshape(-1), grad


def solution(mesh):
    placed = (
        P("cat", "tp"),
        P("cat", "tp"),
        P("cat", "tp"),
        P("tp", None),
        P("cat", None),
        P(),
        P(),
    )
    return jax.shard_map(
        local, mesh=mesh, in_specs=placed, out_specs=(P("cat"), P("cat", "tp")), check_vma=False
    )
```

```python
import functools
import math

import jax
import jax.numpy as jnp
from jax import lax
from jax.experimental import pallas as pl
from jax.experimental.pallas import tpu as pltpu
from jax.sharding import PartitionSpec as P

BLK = 256
LANES = 128
CHUNKS = 4
AHEAD = 3
NEG = -1e30
LOG2E = math.log2(math.e)
LN2 = math.log(2.0)


def lookup(index, values):
    result = values[0]
    for place, value in enumerate(values[1:], 1):
        result = jnp.where(index == place, value, result)
    return result


def nearest(count):
    return [sorted(range(count), key=lambda other: abs(other - at)) for at in range(count)]


def kernel(
    sizes, scale,
    q_ref, pos_in, h_ref, w_ref, bias_ref, loss_ref, grad_ref,
    table, hbuf, wbuf, qbuf, pos_ref, qfull, raw_even, raw_odd, weights, run_max, run_sum, acc, osend, orecv, stats,
    local_sem, w_send, w_recv, w_pass, q_send, q_recv, h_send, h_recv,
    t_send, t_recv, o_send, o_recv, s_send, s_recv,
):
    tp, rows_a, rows_b = sizes
    me_t = lax.axis_index("tp")
    me_c = lax.axis_index("cat")
    core = me_c % 2
    at_b = (me_c // 2) % rows_b
    at_a = me_c // (2 * rows_b)
    queries, width = q_ref.shape
    feats = table.shape[3]
    chunk_rows = table.shape[2]
    own_blocks, _, _ = h_ref.shape
    sub_rows = BLK // tp
    groups = queries // BLK
    part_blocks = own_blocks // CHUNKS
    half = wbuf.shape[2]

    def cat_of(a, b, k):
        return (a * rows_b + b) * 2 + k

    ways = [
        (at_a > 0, cat_of(at_a - 1, at_b, core)),
        (at_a < rows_a - 1, cat_of(at_a + 1, at_b, core)),
        (at_b > 0, cat_of(at_a, at_b - 1, core)),
        (at_b < rows_b - 1, cat_of(at_a, at_b + 1, core)),
        (at_a >= 0, cat_of(at_a, at_b, 1 - core)),
    ]
    peers = [lax.rem(me_t + d, tp) for d in range(1, tp)]

    barrier = pltpu.get_barrier_semaphore()
    total = jnp.int32(tp - 1)
    for peer in peers:
        pl.semaphore_signal(barrier, inc=1, device_id={"tp": peer}, device_id_type=pl.DeviceIdType.MESH)
    for there, target in ways:
        @pl.when(there)
        def _():
            pl.semaphore_signal(barrier, inc=1, device_id={"cat": target}, device_id_type=pl.DeviceIdType.MESH)
        total = total + there.astype(jnp.int32)
    pl.semaphore_wait(barrier, total)

    def across(src, dst, send, recv, peer):
        return pltpu.make_async_remote_copy(
            src_ref=src, dst_ref=dst, send_sem=send, recv_sem=recv,
            device_id={"tp": peer}, device_id_type=pl.DeviceIdType.MESH,
        )

    def w_half(k):
        return w_ref.at[pl.ds(pl.multiple_of(k * half, half), half)]

    def w_copy(slot, d, peer):
        return across(w_half(core), wbuf.at[slot, core], w_send.at[d], w_recv.at[slot, core], peer)

    def w_hand(slot, k, d):
        return pltpu.make_async_remote_copy(
            src_ref=wbuf.at[slot, k], dst_ref=wbuf.at[slot, k],
            send_sem=w_pass.at[d], recv_sem=w_recv.at[slot, k],
            device_id={"cat": ways[4][1]}, device_id_type=pl.DeviceIdType.MESH,
        )

    def q_copy(slot, d, peer):
        return across(q_ref, qbuf.at[slot], q_send.at[d], q_recv.at[slot], peer)

    def h_part(part, owner):
        return h_ref.at[
            pl.ds(part * part_blocks, part_blocks),
            pl.ds(pl.multiple_of(owner * sub_rows, sub_rows), sub_rows),
        ]

    def h_copy(slot, d, part, peer):
        return across(h_part(part, peer), hbuf.at[slot, part], h_send.at[d, part], h_recv.at[slot, part], peer)

    for d, peer in enumerate(peers):
        w_copy(me_t, d, peer).start()
        h_copy(me_t, d, 0, peer).start()
    own = [
        pltpu.make_async_copy(w_half(0), wbuf.at[me_t, 0], local_sem.at[0]),
        pltpu.make_async_copy(w_half(1), wbuf.at[me_t, 1], local_sem.at[1]),
        pltpu.make_async_copy(q_ref, qbuf.at[me_t], local_sem.at[2]),
        pltpu.make_async_copy(pos_in, pos_ref, local_sem.at[3]),
    ]

    def own_part(part):
        return pltpu.make_async_copy(h_part(part, me_t), hbuf.at[me_t, part], local_sem.at[4 + part])

    for copy in own + [own_part(part) for part in range(CHUNKS)]:
        copy.start()

    run_max[...] = jnp.full_like(run_max, NEG)
    run_sum[...] = jnp.zeros_like(run_sum)
    acc[...] = jnp.zeros_like(acc)
    diag = lax.broadcasted_iota(jnp.int32, (LANES, LANES), 0) == lax.broadcasted_iota(
        jnp.int32, (LANES, LANES), 1
    )
    stat_rows = queries // LANES

    def as_row(column):
        return jnp.sum(jnp.where(diag, column, 0.0), axis=0, keepdims=True)

    def as_column(row):
        return jnp.sum(jnp.where(diag, row, 0.0), axis=1, keepdims=True)

    def pair_of(a, b, part):
        return (a * rows_b + b) * CHUNKS + part

    def table_copy(pair, k, way):
        return pltpu.make_async_remote_copy(
            src_ref=table.at[pair, k], dst_ref=table.at[pair, k],
            send_sem=t_send.at[pair, way], recv_sem=t_recv.at[pair, k],
            device_id={"cat": ways[way][1]}, device_id_type=pl.DeviceIdType.MESH,
        )

    def sends(a, b, part):
        b_first = (part == 2) & (a != rows_a // 2)
        along_a = b_first | (b == at_b)
        along_b = jnp.logical_not(b_first) | (a == at_a)
        return [
            ways[0][0] & along_a & (a >= at_a),
            ways[1][0] & along_a & (a <= at_a),
            ways[2][0] & along_b & (b >= at_b),
            ways[3][0] & along_b & (b <= at_b),
            ways[4][0],
        ]

    def hand_on(a, b, part, act):
        pair = pair_of(a, b, part)
        for way, wanted in enumerate(sends(a, b, part)):
            @pl.when(wanted)
            def _():
                act(table_copy(pair, core, way))

    order = sorted(
        [(i, j, p) for p in range(CHUNKS) for i in range(rows_a) for j in range(rows_b)],
        key=lambda r: (r[0] + r[1] + (rows_a - 0.5) * r[2], r[1]),
    )
    near_a, near_b = nearest(rows_a), nearest(rows_b)

    def source(step):
        rank_a, rank_b, part = (lookup(step, [r[i] for r in order]) for i in range(3))
        a = lookup(rank_a * rows_a + at_a, [near_a[p][r] for r in range(rows_a) for p in range(rows_a)])
        b = lookup(rank_b * rows_b + at_b, [near_b[p][r] for r in range(rows_b) for p in range(rows_b)])
        return a, b, part

    def advance(step):
        a, b, part = source(step)
        mine = (a == at_a) & (b == at_b)

        @pl.when(mine)
        def _():
            own_part(part).wait()
            for d, peer in enumerate(peers):
                h_copy(peer, d, part, peer).wait_recv()
            vec = jnp.zeros((chunk_rows, feats), jnp.float32)
            for t in range(tp):
                for k in range(2):
                    hidden = hbuf[t, part, :, :, k * half:(k + 1) * half]
                    vec = vec + jnp.dot(
                        hidden.reshape(chunk_rows, half), wbuf[t, k], preferred_element_type=jnp.float32
                    )
            table[pair_of(a, b, part), core] = vec.astype(jnp.bfloat16)

        @pl.when(jnp.logical_not(mine))
        def _():
            table_copy(pair_of(a, b, part), core, 4).wait_recv()

        hand_on(a, b, part, lambda copy: copy.start())

    def partner(step):
        pair = pair_of(*source(step))
        table_copy(pair, 1 - core, 4).wait_recv()
        return pair

    own[0].wait()
    own[1].wait()
    for d, peer in enumerate(peers):
        w_copy(peer, d, peer).wait_recv()
        w_hand(peer, core, d).start()
    for d, peer in enumerate(peers):
        w_hand(peer, 1 - core, d).wait_recv()
    advance(jnp.int32(0))
    for d, peer in enumerate(peers):
        q_copy(me_t, d, peer).start()
    for d, peer in enumerate(peers):
        h_copy(me_t, d, 1, peer).start()

    @pl.loop(1, AHEAD)
    def _(step):
        advance(step)

    own[2].wait()
    own[3].wait()
    for d, peer in enumerate(peers):
        q_copy(peer, d, peer).wait_recv()
    for part in range(2, CHUNKS):
        for d, peer in enumerate(peers):
            h_copy(me_t, d, part, peer).start()
    for t in range(tp):
        qfull[:, t * width:(t + 1) * width] = qbuf[t]

    def score(pair, raw):
        items = table[pair].reshape(2 * chunk_rows, feats)
        raw[...] = lax.dot_general(
            qfull[...], items, (((1,), (1,)), ((), ())), preferred_element_type=jnp.float32
        )

    def absorb(pair, raw):
        fades = []
        for g in range(groups):
            rows = slice(g * BLK, (g + 1) * BLK)
            tiles = [
                raw[rows, i * LANES:(i + 1) * LANES] * (scale * LOG2E) + bias_ref[g, pair, i:i + 1, :]
                for i in range(2 * chunk_rows // LANES)
            ]
            top = functools.reduce(jnp.maximum, tiles)
            old_max = run_max[rows, :]
            new_max = jnp.maximum(old_max, jnp.max(top, axis=1, keepdims=True))
            fade = jnp.exp2(old_max - new_max)
            tiles = [jnp.exp2(tile - new_max) for tile in tiles]
            run_max[rows, :] = new_max
            run_sum[rows, :] = run_sum[rows, :] * fade + functools.reduce(jnp.add, tiles)
            for i, tile in enumerate(tiles):
                weights[rows, i * LANES:(i + 1) * LANES] = tile.astype(jnp.bfloat16)
            fades.append(fade)
        items = table[pair].reshape(2 * chunk_rows, feats)
        part = jnp.dot(weights[...], items, preferred_element_type=jnp.float32)
        for g in range(groups):
            rows = slice(g * BLK, (g + 1) * BLK)
            for i in range(feats // LANES):
                cols = slice(i * LANES, (i + 1) * LANES)
                acc[rows, cols] = acc[rows, cols] * fades[g] + part[rows, cols]

    steps = len(order)

    first = partner(jnp.int32(0))
    score(first, raw_even)

    @pl.loop(0, steps // 2 - 1)
    def _(twice):
        step = twice * 2
        for later, raw, raw_next in ((0, raw_even, raw_odd), (1, raw_odd, raw_even)):
            @pl.when(step + later + AHEAD < steps)
            def _():
                advance(step + later + AHEAD)

            coming = partner(step + later + 1)
            score(coming, raw_next)
            absorb(pair_of(*source(step + later)), raw)

    last = partner(jnp.int32(steps - 1))
    score(last, raw_odd)
    absorb(pair_of(*source(jnp.int32(steps - 2))), raw_even)
    for row in range(stat_rows):
        rows = slice(row * LANES, (row + 1) * LANES)
        product = qbuf[me_t, rows, :].astype(jnp.float32) * pos_ref[rows, :].astype(jnp.float32)
        stats[me_t, stat_rows + row:stat_rows + row + 1, :] = as_row(
            jnp.sum(product, axis=1, keepdims=True)
        )
    absorb(last, raw_odd)

    def o_copy(slot, d, g, peer):
        rows = pl.ds(g * BLK, BLK)
        return across(osend.at[d, rows], orecv.at[slot, rows], o_send.at[d, g], o_recv.at[slot, g], peer)

    def s_copy(slot, d, peer):
        return across(stats.at[slot], stats.at[slot], s_send.at[d], s_recv.at[slot], peer)

    for g in range(groups):
        rows = slice(g * BLK, (g + 1) * BLK)
        norm = jnp.sum(run_sum[rows, :], axis=1, keepdims=True)
        lse = run_max[rows, 0:1] + jnp.log2(norm)
        inverse = 1.0 / norm
        for i in range(BLK // LANES):
            row = g * (BLK // LANES) + i
            stats[me_t, row:row + 1, :] = as_row(lse[i * LANES:(i + 1) * LANES, :])
        for d, peer in enumerate(peers):
            cols = pl.ds(pl.multiple_of(peer * width, LANES), width)
            osend[d, rows, :] = (acc[rows, cols] * inverse).astype(jnp.bfloat16)
            o_copy(me_t, d, g, peer).start()
        cols = pl.ds(pl.multiple_of(me_t * width, LANES), width)
        acc[rows, cols] = acc[rows, cols] * inverse
    for d, peer in enumerate(peers):
        s_copy(me_t, d, peer).start()
    for d, peer in enumerate(peers):
        s_copy(peer, d, peer).wait_recv()
    for g in range(groups):
        for d, peer in enumerate(peers):
            o_copy(peer, d, g, peer).wait_recv()
        for i in range(BLK // LANES):
            row = g * (BLK // LANES) + i
            rows = slice(row * LANES, (row + 1) * LANES)
            pos = sum(stats[t, stat_rows + row:stat_rows + row + 1, :] for t in range(tp)) * (scale * LOG2E)
            lses = [stats[t, row:row + 1, :] for t in range(tp)]
            top = functools.reduce(jnp.maximum, lses + [pos])
            log_total = top + jnp.log2(sum(jnp.exp2(v - top) for v in lses + [pos]))
            loss_ref[row:row + 1, :] = (log_total - pos) * LN2
            shift = as_column(log_total)
            cols = pl.ds(pl.multiple_of(me_t * width, LANES), width)
            grad = acc[rows, cols] * jnp.exp2(as_column(stats[me_t, row:row + 1, :]) - shift)
            for peer in peers:
                share = jnp.exp2(as_column(stats[peer, row:row + 1, :]) - shift)
                grad = grad + orecv[peer, rows, :].astype(jnp.float32) * share
            pos_weight = jnp.exp2(as_column(pos - log_total)) - 1.0
            grad = grad + pos_weight * pos_ref[rows, :].astype(jnp.float32)
            grad_ref[rows, :] = (scale * grad).astype(jnp.bfloat16)

    for d, peer in enumerate(peers):
        w_copy(me_t, d, peer).wait_send()
        w_hand(peer, core, d).wait_send()
        q_copy(me_t, d, peer).wait_send()
        for part in range(CHUNKS):
            h_copy(me_t, d, part, peer).wait_send()
        for g in range(groups):
            o_copy(me_t, d, g, peer).wait_send()
        s_copy(me_t, d, peer).wait_send()

    @pl.loop(0, steps)
    def _(step):
        hand_on(*source(step), lambda copy: copy.wait_send())


def local(query_emb, positive_emb, item_hidden, item_weight, neg_blocks, block_home, sample_counts):
    tp = lax.axis_size("tp")
    cats = lax.axis_size("cat")
    rows_a = 4
    rows_b = cats // 2 // rows_a
    me_t = lax.axis_index("tp")
    queries, width = query_emb.shape
    hid, feats = item_weight.shape
    own_blocks = item_hidden.shape[0] // BLK
    sub_rows = BLK // tp
    total_blocks = block_home.shape[0]
    groups = neg_blocks.shape[0]
    chunk_rows = own_blocks * sub_rows // CHUNKS
    pairs = cats // 2 * CHUNKS
    scale = 2.0 / math.sqrt(feats)

    ids = jnp.arange(total_blocks, dtype=jnp.int32)
    chosen = jnp.any(neg_blocks[:, :, None] == ids, axis=1)
    stored = jnp.any(chosen[:, :, None] & (block_home[:, None] == ids), axis=1)
    log_q = jnp.log(sample_counts.astype(jnp.float32)).reshape(total_blocks, tp, sub_rows)
    log_q = lax.dynamic_index_in_dim(log_q, me_t, 1, keepdims=False)
    bias = jnp.where(stored[:, :, None], log_q * -LOG2E, NEG)
    bias = (
        bias.reshape(groups, cats // 2, 2, CHUNKS, chunk_rows)
        .transpose(0, 1, 3, 2, 4)
        .reshape(groups, pairs, 2 * chunk_rows // LANES, LANES)
    )
    vmem = pl.BlockSpec(memory_space=pltpu.VMEM)
    hbm = pl.BlockSpec(memory_space=pl.ANY)
    dma = pltpu.SemaphoreType.DMA
    others = max(tp - 1, 1)
    pairwise = queries * pairs * 2 * chunk_rows
    loss, grad = pl.pallas_call(
        functools.partial(kernel, (tp, rows_a, rows_b), scale),
        out_shape=(
            jax.ShapeDtypeStruct((queries // LANES, LANES), jnp.float32),
            jax.ShapeDtypeStruct((queries, width), jnp.bfloat16),
        ),
        in_specs=[hbm, hbm, hbm, hbm, vmem],
        out_specs=(vmem, vmem),
        scratch_shapes=[
            pltpu.VMEM((pairs, 2, chunk_rows, feats), jnp.bfloat16),
            pltpu.VMEM((tp, CHUNKS, own_blocks // CHUNKS, sub_rows, hid), jnp.bfloat16),
            pltpu.VMEM((tp, 2, hid // 2, feats), jnp.bfloat16),
            pltpu.VMEM((tp, queries, width), jnp.bfloat16),
            pltpu.VMEM((queries, width), jnp.bfloat16),
            pltpu.VMEM((queries, feats), jnp.bfloat16),
            pltpu.VMEM((queries, 2 * chunk_rows), jnp.float32),
            pltpu.VMEM((queries, 2 * chunk_rows), jnp.float32),
            pltpu.VMEM((queries, 2 * chunk_rows), jnp.bfloat16),
            pltpu.VMEM((queries, LANES), jnp.float32),
            pltpu.VMEM((queries, LANES), jnp.float32),
            pltpu.VMEM((queries, feats), jnp.float32),
            pltpu.VMEM((others, queries, width), jnp.bfloat16),
            pltpu.VMEM((tp, queries, width), jnp.bfloat16),
            pltpu.VMEM((tp, 2 * queries // LANES, LANES), jnp.float32),
            dma((4 + CHUNKS,)),
            dma((others,)), dma((tp, 2)), dma((others,)),
            dma((others,)), dma((tp,)),
            dma((others, CHUNKS)), dma((tp, CHUNKS)),
            dma((pairs, 5)), dma((pairs, 2)),
            dma((others, groups)), dma((tp, groups)),
            dma((others,)), dma((tp,)),
        ],
        compiler_params=pltpu.CompilerParams(
            collective_id=0, has_side_effects=True, vmem_limit_bytes=60 * 1024 * 1024
        ),
        cost_estimate=pl.CostEstimate(
            flops=4 * pairwise * feats, bytes_accessed=8 * 1024 * 1024, transcendentals=pairwise
        ),
    )(
        query_emb, positive_emb, item_hidden.reshape(own_blocks, BLK, hid), item_weight, bias,
    )
    return loss.reshape(-1), grad


def solution(mesh):
    placed = (
        P("cat", "tp"),
        P("cat", "tp"),
        P("cat", "tp"),
        P("tp", None),
        P("cat", None),
        P(),
        P(),
    )
    return jax.shard_map(
        local, mesh=mesh, in_specs=placed, out_specs=(P("cat"), P("cat", "tp")), check_vma=False
    )
```

```python
import functools
import math

import jax
import jax.numpy as jnp
from jax import lax
from jax.experimental import pallas as pl
from jax.experimental.pallas import tpu as pltpu
from jax.sharding import PartitionSpec as P

BLK = 256
LANES = 128
CHUNKS = 4
AHEAD = 3
NEG = -1e30
LOG2E = math.log2(math.e)
LN2 = math.log(2.0)


def lookup(index, values):
    result = values[0]
    for place, value in enumerate(values[1:], 1):
        result = jnp.where(index == place, value, result)
    return result


def nearest(count):
    return [sorted(range(count), key=lambda other: abs(other - at)) for at in range(count)]


def kernel(
    sizes, scale,
    q_ref, pos_in, h_ref, w_ref, bias_ref, loss_ref, grad_ref,
    table, hbuf, wbuf, qbuf, pos_ref, qfull, raw_even, raw_odd, weights, run_max, run_sum, acc, osend, orecv, stats,
    local_sem, w_send, w_recv, w_pass, q_send, q_recv, h_send, h_recv,
    t_send, t_recv, o_send, o_recv, s_send, s_recv,
):
    tp, rows_a, rows_b = sizes
    me_t = lax.axis_index("tp")
    me_c = lax.axis_index("cat")
    core = me_c % 2
    at_b = (me_c // 2) % rows_b
    at_a = me_c // (2 * rows_b)
    queries, width = q_ref.shape
    feats = table.shape[3]
    chunk_rows = table.shape[2]
    own_blocks, _, _ = h_ref.shape
    sub_rows = BLK // tp
    groups = queries // BLK
    part_blocks = own_blocks // CHUNKS
    half = wbuf.shape[2]

    def cat_of(a, b, k):
        return (a * rows_b + b) * 2 + k

    ways = [
        (at_a > 0, cat_of(at_a - 1, at_b, core)),
        (at_a < rows_a - 1, cat_of(at_a + 1, at_b, core)),
        (at_b > 0, cat_of(at_a, at_b - 1, core)),
        (at_b < rows_b - 1, cat_of(at_a, at_b + 1, core)),
        (at_a >= 0, cat_of(at_a, at_b, 1 - core)),
    ]
    peers = [lax.rem(me_t + d, tp) for d in range(1, tp)]

    barrier = pltpu.get_barrier_semaphore()
    total = jnp.int32(tp - 1)
    for peer in peers:
        pl.semaphore_signal(barrier, inc=1, device_id={"tp": peer}, device_id_type=pl.DeviceIdType.MESH)
    for there, target in ways:
        @pl.when(there)
        def _():
            pl.semaphore_signal(barrier, inc=1, device_id={"cat": target}, device_id_type=pl.DeviceIdType.MESH)
        total = total + there.astype(jnp.int32)
    pl.semaphore_wait(barrier, total)

    def across(src, dst, send, recv, peer):
        return pltpu.make_async_remote_copy(
            src_ref=src, dst_ref=dst, send_sem=send, recv_sem=recv,
            device_id={"tp": peer}, device_id_type=pl.DeviceIdType.MESH,
        )

    def w_half(k):
        return w_ref.at[pl.ds(pl.multiple_of(k * half, half), half)]

    def w_copy(slot, d, peer):
        return across(w_half(core), wbuf.at[slot, core], w_send.at[d], w_recv.at[slot, core], peer)

    def w_hand(slot, k, d):
        return pltpu.make_async_remote_copy(
            src_ref=wbuf.at[slot, k], dst_ref=wbuf.at[slot, k],
            send_sem=w_pass.at[d], recv_sem=w_recv.at[slot, k],
            device_id={"cat": ways[4][1]}, device_id_type=pl.DeviceIdType.MESH,
        )

    def q_copy(slot, d, peer):
        return across(q_ref, qbuf.at[slot], q_send.at[d], q_recv.at[slot], peer)

    def h_part(part, owner):
        return h_ref.at[
            pl.ds(part * part_blocks, part_blocks),
            pl.ds(pl.multiple_of(owner * sub_rows, sub_rows), sub_rows),
        ]

    def h_copy(slot, d, part, peer):
        return across(h_part(part, peer), hbuf.at[slot, part], h_send.at[d, part], h_recv.at[slot, part], peer)

    for d, peer in enumerate(peers):
        w_copy(me_t, d, peer).start()
        h_copy(me_t, d, 0, peer).start()
    own = [
        pltpu.make_async_copy(w_half(0), wbuf.at[me_t, 0], local_sem.at[0]),
        pltpu.make_async_copy(w_half(1), wbuf.at[me_t, 1], local_sem.at[1]),
        pltpu.make_async_copy(q_ref, qbuf.at[me_t], local_sem.at[2]),
        pltpu.make_async_copy(pos_in, pos_ref, local_sem.at[3]),
    ]

    def own_part(part):
        return pltpu.make_async_copy(h_part(part, me_t), hbuf.at[me_t, part], local_sem.at[4 + part])

    for copy in own + [own_part(part) for part in range(CHUNKS)]:
        copy.start()

    run_max[...] = jnp.full_like(run_max, NEG)
    run_sum[...] = jnp.zeros_like(run_sum)
    acc[...] = jnp.zeros_like(acc)
    diag = lax.broadcasted_iota(jnp.int32, (LANES, LANES), 0) == lax.broadcasted_iota(
        jnp.int32, (LANES, LANES), 1
    )
    stat_rows = queries // LANES

    def as_row(column):
        return jnp.sum(jnp.where(diag, column, 0.0), axis=0, keepdims=True)

    def as_column(row):
        return jnp.sum(jnp.where(diag, row, 0.0), axis=1, keepdims=True)

    def pair_of(a, b, part):
        return (a * rows_b + b) * CHUNKS + part

    def table_copy(pair, k, way):
        return pltpu.make_async_remote_copy(
            src_ref=table.at[pair, k], dst_ref=table.at[pair, k],
            send_sem=t_send.at[pair, way], recv_sem=t_recv.at[pair, k],
            device_id={"cat": ways[way][1]}, device_id_type=pl.DeviceIdType.MESH,
        )

    def sends(a, b):
        along_a = b == at_b
        return [
            ways[0][0] & along_a & (a >= at_a),
            ways[1][0] & along_a & (a <= at_a),
            ways[2][0] & (b >= at_b),
            ways[3][0] & (b <= at_b),
            ways[4][0],
        ]

    def hand_on(a, b, part, act):
        pair = pair_of(a, b, part)
        for way, wanted in enumerate(sends(a, b)):
            @pl.when(wanted)
            def _():
                act(table_copy(pair, core, way))

    order = sorted(
        [(i, j, p) for p in range(CHUNKS) for i in range(rows_a) for j in range(rows_b)],
        key=lambda r: (r[0] + r[1] + (rows_a - 0.5) * r[2], r[1]),
    )
    near_a, near_b = nearest(rows_a), nearest(rows_b)

    def source(step):
        rank_a, rank_b, part = (lookup(step, [r[i] for r in order]) for i in range(3))
        a = lookup(rank_a * rows_a + at_a, [near_a[p][r] for r in range(rows_a) for p in range(rows_a)])
        b = lookup(rank_b * rows_b + at_b, [near_b[p][r] for r in range(rows_b) for p in range(rows_b)])
        return a, b, part

    def advance(step):
        a, b, part = source(step)
        mine = (a == at_a) & (b == at_b)

        @pl.when(mine)
        def _():
            own_part(part).wait()
            for d, peer in enumerate(peers):
                h_copy(peer, d, part, peer).wait_recv()
            vec = jnp.zeros((chunk_rows, feats), jnp.float32)
            for t in range(tp):
                for k in range(2):
                    hidden = hbuf[t, part, :, :, k * half:(k + 1) * half]
                    vec = vec + jnp.dot(
                        hidden.reshape(chunk_rows, half), wbuf[t, k], preferred_element_type=jnp.float32
                    )
            table[pair_of(a, b, part), core] = vec.astype(jnp.bfloat16)

        @pl.when(jnp.logical_not(mine))
        def _():
            table_copy(pair_of(a, b, part), core, 4).wait_recv()

        hand_on(a, b, part, lambda copy: copy.start())

    def partner(step):
        pair = pair_of(*source(step))
        table_copy(pair, 1 - core, 4).wait_recv()
        return pair

    own[0].wait()
    own[1].wait()
    for d, peer in enumerate(peers):
        w_copy(peer, d, peer).wait_recv()
        w_hand(peer, core, d).start()
    for d, peer in enumerate(peers):
        w_hand(peer, 1 - core, d).wait_recv()
    advance(jnp.int32(0))
    for d, peer in enumerate(peers):
        q_copy(me_t, d, peer).start()
    for d, peer in enumerate(peers):
        h_copy(me_t, d, 1, peer).start()

    @pl.loop(1, AHEAD)
    def _(step):
        advance(step)

    own[2].wait()
    own[3].wait()
    for d, peer in enumerate(peers):
        q_copy(peer, d, peer).wait_recv()
    for part in range(2, CHUNKS):
        for d, peer in enumerate(peers):
            h_copy(me_t, d, part, peer).start()
    for t in range(tp):
        qfull[:, t * width:(t + 1) * width] = qbuf[t]

    def score(pair, raw):
        items = table[pair].reshape(2 * chunk_rows, feats)
        raw[...] = lax.dot_general(
            qfull[...], items, (((1,), (1,)), ((), ())), preferred_element_type=jnp.float32
        )

    def absorb(pair, raw):
        fades = []
        for g in range(groups):
            rows = slice(g * BLK, (g + 1) * BLK)
            tiles = [
                raw[rows, i * LANES:(i + 1) * LANES] * (scale * LOG2E) + bias_ref[g, pair, i:i + 1, :]
                for i in range(2 * chunk_rows // LANES)
            ]
            top = functools.reduce(jnp.maximum, tiles)
            old_max = run_max[rows, :]
            new_max = jnp.maximum(old_max, jnp.max(top, axis=1, keepdims=True))
            fade = jnp.exp2(old_max - new_max)
            tiles = [jnp.exp2(tile - new_max) for tile in tiles]
            run_max[rows, :] = new_max
            run_sum[rows, :] = run_sum[rows, :] * fade + functools.reduce(jnp.add, tiles)
            for i, tile in enumerate(tiles):
                weights[rows, i * LANES:(i + 1) * LANES] = tile.astype(jnp.bfloat16)
            fades.append(fade)
        items = table[pair].reshape(2 * chunk_rows, feats)
        part = jnp.dot(weights[...], items, preferred_element_type=jnp.float32)
        for g in range(groups):
            rows = slice(g * BLK, (g + 1) * BLK)
            for i in range(feats // LANES):
                cols = slice(i * LANES, (i + 1) * LANES)
                acc[rows, cols] = acc[rows, cols] * fades[g] + part[rows, cols]

    steps = len(order)

    first = partner(jnp.int32(0))
    score(first, raw_even)

    @pl.loop(0, steps // 2 - 1)
    def _(twice):
        step = twice * 2
        for later, raw, raw_next in ((0, raw_even, raw_odd), (1, raw_odd, raw_even)):
            @pl.when(step + later + AHEAD < steps)
            def _():
                advance(step + later + AHEAD)

            coming = partner(step + later + 1)
            score(coming, raw_next)
            absorb(pair_of(*source(step + later)), raw)

    last = partner(jnp.int32(steps - 1))
    score(last, raw_odd)
    absorb(pair_of(*source(jnp.int32(steps - 2))), raw_even)
    for row in range(stat_rows):
        rows = slice(row * LANES, (row + 1) * LANES)
        product = qbuf[me_t, rows, :].astype(jnp.float32) * pos_ref[rows, :].astype(jnp.float32)
        stats[me_t, stat_rows + row:stat_rows + row + 1, :] = as_row(
            jnp.sum(product, axis=1, keepdims=True)
        )
    absorb(last, raw_odd)

    def o_copy(slot, d, g, peer):
        rows = pl.ds(g * BLK, BLK)
        return across(osend.at[d, rows], orecv.at[slot, rows], o_send.at[d, g], o_recv.at[slot, g], peer)

    def s_copy(slot, d, peer):
        return across(stats.at[slot], stats.at[slot], s_send.at[d], s_recv.at[slot], peer)

    for g in range(groups):
        rows = slice(g * BLK, (g + 1) * BLK)
        norm = jnp.sum(run_sum[rows, :], axis=1, keepdims=True)
        lse = run_max[rows, 0:1] + jnp.log2(norm)
        inverse = 1.0 / norm
        for i in range(BLK // LANES):
            row = g * (BLK // LANES) + i
            stats[me_t, row:row + 1, :] = as_row(lse[i * LANES:(i + 1) * LANES, :])
        for d, peer in enumerate(peers):
            cols = pl.ds(pl.multiple_of(peer * width, LANES), width)
            osend[d, rows, :] = (acc[rows, cols] * inverse).astype(jnp.bfloat16)
            o_copy(me_t, d, g, peer).start()
        cols = pl.ds(pl.multiple_of(me_t * width, LANES), width)
        acc[rows, cols] = acc[rows, cols] * inverse
    for d, peer in enumerate(peers):
        s_copy(me_t, d, peer).start()
    for d, peer in enumerate(peers):
        s_copy(peer, d, peer).wait_recv()
    for g in range(groups):
        for d, peer in enumerate(peers):
            o_copy(peer, d, g, peer).wait_recv()
        for i in range(BLK // LANES):
            row = g * (BLK // LANES) + i
            rows = slice(row * LANES, (row + 1) * LANES)
            pos = sum(stats[t, stat_rows + row:stat_rows + row + 1, :] for t in range(tp)) * (scale * LOG2E)
            lses = [stats[t, row:row + 1, :] for t in range(tp)]
            top = functools.reduce(jnp.maximum, lses + [pos])
            log_total = top + jnp.log2(sum(jnp.exp2(v - top) for v in lses + [pos]))
            loss_ref[row:row + 1, :] = (log_total - pos) * LN2
            shift = as_column(log_total)
            cols = pl.ds(pl.multiple_of(me_t * width, LANES), width)
            grad = acc[rows, cols] * jnp.exp2(as_column(stats[me_t, row:row + 1, :]) - shift)
            for peer in peers:
                share = jnp.exp2(as_column(stats[peer, row:row + 1, :]) - shift)
                grad = grad + orecv[peer, rows, :].astype(jnp.float32) * share
            pos_weight = jnp.exp2(as_column(pos - log_total)) - 1.0
            grad = grad + pos_weight * pos_ref[rows, :].astype(jnp.float32)
            grad_ref[rows, :] = (scale * grad).astype(jnp.bfloat16)

    for d, peer in enumerate(peers):
        w_copy(me_t, d, peer).wait_send()
        w_hand(peer, core, d).wait_send()
        q_copy(me_t, d, peer).wait_send()
        for part in range(CHUNKS):
            h_copy(me_t, d, part, peer).wait_send()
        for g in range(groups):
            o_copy(me_t, d, g, peer).wait_send()
        s_copy(me_t, d, peer).wait_send()

    @pl.loop(0, steps)
    def _(step):
        hand_on(*source(step), lambda copy: copy.wait_send())


def local(query_emb, positive_emb, item_hidden, item_weight, neg_blocks, block_home, sample_counts):
    tp = lax.axis_size("tp")
    cats = lax.axis_size("cat")
    rows_a = 4
    rows_b = cats // 2 // rows_a
    me_t = lax.axis_index("tp")
    queries, width = query_emb.shape
    hid, feats = item_weight.shape
    own_blocks = item_hidden.shape[0] // BLK
    sub_rows = BLK // tp
    total_blocks = block_home.shape[0]
    groups = neg_blocks.shape[0]
    chunk_rows = own_blocks * sub_rows // CHUNKS
    pairs = cats // 2 * CHUNKS
    scale = 2.0 / math.sqrt(feats)

    ids = jnp.arange(total_blocks, dtype=jnp.int32)
    chosen = jnp.any(neg_blocks[:, :, None] == ids, axis=1)
    stored = jnp.any(chosen[:, :, None] & (block_home[:, None] == ids), axis=1)
    log_q = jnp.log(sample_counts.astype(jnp.float32)).reshape(total_blocks, tp, sub_rows)
    log_q = lax.dynamic_index_in_dim(log_q, me_t, 1, keepdims=False)
    bias = jnp.where(stored[:, :, None], log_q * -LOG2E, NEG)
    bias = (
        bias.reshape(groups, cats // 2, 2, CHUNKS, chunk_rows)
        .transpose(0, 1, 3, 2, 4)
        .reshape(groups, pairs, 2 * chunk_rows // LANES, LANES)
    )
    vmem = pl.BlockSpec(memory_space=pltpu.VMEM)
    hbm = pl.BlockSpec(memory_space=pl.ANY)
    dma = pltpu.SemaphoreType.DMA
    others = max(tp - 1, 1)
    pairwise = queries * pairs * 2 * chunk_rows
    loss, grad = pl.pallas_call(
        functools.partial(kernel, (tp, rows_a, rows_b), scale),
        out_shape=(
            jax.ShapeDtypeStruct((queries // LANES, LANES), jnp.float32),
            jax.ShapeDtypeStruct((queries, width), jnp.bfloat16),
        ),
        in_specs=[hbm, hbm, hbm, hbm, vmem],
        out_specs=(vmem, vmem),
        scratch_shapes=[
            pltpu.VMEM((pairs, 2, chunk_rows, feats), jnp.bfloat16),
            pltpu.VMEM((tp, CHUNKS, own_blocks // CHUNKS, sub_rows, hid), jnp.bfloat16),
            pltpu.VMEM((tp, 2, hid // 2, feats), jnp.bfloat16),
            pltpu.VMEM((tp, queries, width), jnp.bfloat16),
            pltpu.VMEM((queries, width), jnp.bfloat16),
            pltpu.VMEM((queries, feats), jnp.bfloat16),
            pltpu.VMEM((queries, 2 * chunk_rows), jnp.float32),
            pltpu.VMEM((queries, 2 * chunk_rows), jnp.float32),
            pltpu.VMEM((queries, 2 * chunk_rows), jnp.bfloat16),
            pltpu.VMEM((queries, LANES), jnp.float32),
            pltpu.VMEM((queries, LANES), jnp.float32),
            pltpu.VMEM((queries, feats), jnp.float32),
            pltpu.VMEM((others, queries, width), jnp.bfloat16),
            pltpu.VMEM((tp, queries, width), jnp.bfloat16),
            pltpu.VMEM((tp, 2 * queries // LANES, LANES), jnp.float32),
            dma((4 + CHUNKS,)),
            dma((others,)), dma((tp, 2)), dma((others,)),
            dma((others,)), dma((tp,)),
            dma((others, CHUNKS)), dma((tp, CHUNKS)),
            dma((pairs, 5)), dma((pairs, 2)),
            dma((others, groups)), dma((tp, groups)),
            dma((others,)), dma((tp,)),
        ],
        compiler_params=pltpu.CompilerParams(
            collective_id=0, has_side_effects=True, vmem_limit_bytes=60 * 1024 * 1024
        ),
        cost_estimate=pl.CostEstimate(
            flops=4 * pairwise * feats, bytes_accessed=8 * 1024 * 1024, transcendentals=pairwise
        ),
    )(
        query_emb, positive_emb, item_hidden.reshape(own_blocks, BLK, hid), item_weight, bias,
    )
    return loss.reshape(-1), grad


def solution(mesh):
    placed = (
        P("cat", "tp"),
        P("cat", "tp"),
        P("cat", "tp"),
        P("tp", None),
        P("cat", None),
        P(),
        P(),
    )
    return jax.shard_map(
        local, mesh=mesh, in_specs=placed, out_specs=(P("cat"), P("cat", "tp")), check_vma=False
    )
```
